128 devices in a mesh: gx: 8 (over z, core), gy: 16 (over x, y).
Axes of the slice: x: 4, y: 4, z: 4, core: 2. Of those that a mesh axis runs over, the one named last changes fastest.
Arguments:
- tokens: bfloat16 [200704, 1024], P(('gx', 'gy')), may hold values from -6 to 6
- image_slot: int32 [1024], replicated, may hold values from 0 to 1023, as said below
- pairs: int32 [1024, 2], P(('gx', 'gy')), may hold values from 0 to 1023, as said below
- w_embed: bfloat16 [1024, 768], replicated, may hold values from -0.1875 to 0.1875
- gain_query: float32 [768], replicated, may hold values from 0.1 to 1.9
- gain_key: float32 [768], replicated, may hold values from 0.1 to 1.9
- w_query: bfloat16 [768, 768], replicated, may hold values from -0.21875 to 0.21875
- w_key: bfloat16 [768, 768], replicated, may hold values from -0.21875 to 0.21875
- w_value: bfloat16 [768, 768], replicated, may hold values from -0.21875 to 0.21875
- w_out: bfloat16 [768, 768], replicated, may hold values from -0.21875 to 0.21875
- gain_head: float32 [768], replicated, may hold values from 0.1 to 1.9
- w_head: bfloat16 [768, 1024], replicated, may hold values from -0.21875 to 0.21875
Outputs:
- point_sums: float32 [200704, 1024], P(('gx', 'gy'))
The draws below stay inside these ranges and needn't reach their ends.
Inputs may be any that keep to these rules, and one draw needn't show every extreme that they name: `image_slot`: A permutation: each slot holds one image. Device w = a * 16 + b (gx index a, gy index b) holds pairs w * 8 to (w + 1) * 8 - 1. The device owning slot s is s // 8. For every pair of device (a, b), its first image's owner has gx index a and its second image's owner has gy index b. The first images of one device's pairs have owners of different gy indices (1 at most per owner); the second images have at most 2 owners alike in gx index, exactly 2 for some. The two images of a pair differ.
All inputs are finite; a program needn't handle non-finite values.
Results may differ from the reference program's by a relative error of at most 0.011.
Values may be sent and summed in bfloat16 or wider, within the bound.
A program may use at most 256 MiB of HBM per device.

```python
import jax
import jax.numpy as jnp
from jax import lax

D_ENC = 1024
D_MODEL = 768
HEADS = 12
PATCHES = 196
PIXELS = 256
HEAD_OUT = 1024
IMG_DEV = 8
IMAGES = 1024
PAIR_DEV = 8
PAIRS = 1024
N_GX = 8
N_GY = 16


def routing(key):
    workers = N_GX * N_GY
    slot_of = jax.random.permutation(jax.random.fold_in(key, 101), IMAGES).astype(jnp.int32)
    image_at = jnp.zeros((IMAGES,), jnp.int32).at[slot_of].set(jnp.arange(IMAGES, dtype=jnp.int32))
    worker_keys = jax.random.split(jax.random.fold_in(key, 102), workers)

    def worker_pairs(sub, index):
        keys = jax.random.split(sub, 5)
        own_row = index // N_GY
        own_col = index % N_GY
        first_col = jax.random.permutation(keys[0], N_GY)[:PAIR_DEV].astype(jnp.int32)
        second_row = jax.random.permutation(keys[1], N_GX)[jnp.arange(PAIR_DEV) % (PAIR_DEV // 2)].astype(jnp.int32)
        order = jax.random.permutation(keys[2], PAIR_DEV)
        first_col = first_col[order]
        second_row = second_row[order]
        first_local = jax.random.randint(keys[3], (PAIR_DEV,), 0, IMG_DEV).astype(jnp.int32)
        second_local = jax.random.randint(keys[4], (PAIR_DEV,), 0, IMG_DEV).astype(jnp.int32)
        first_slot = (own_row * N_GY + first_col) * IMG_DEV + first_local
        second_base = (second_row * N_GY + own_col) * IMG_DEV
        second_slot = second_base + second_local
        second_slot = jnp.where(first_slot == second_slot, second_base + (second_local + 1) % IMG_DEV, second_slot)
        return jnp.stack([first_slot, second_slot], axis=1).astype(jnp.int32)
    slot_pairs = jax.vmap(worker_pairs)(worker_keys, jnp.arange(workers, dtype=jnp.int32))
    slot_pairs = slot_pairs.reshape(workers * PAIR_DEV, 2)
    return (slot_of, image_at[slot_pairs].astype(jnp.int32))


def draw_image_slot(key, part):
    return routing(key)[0]


def draw_pairs(key, part):
    return routing(key)[1]


def levels(key, dims, cuts, smallest, high):
    def one(position, shards_of):
        steps = jax.random.uniform(jax.random.fold_in(jax.random.fold_in(key, 6), position), (shards_of,), jnp.float32, smallest / len(cuts), high / len(cuts))
        return jnp.repeat(jnp.exp(steps), dims[position] // shards_of).reshape((-1,) + (1,) * (len(dims) - position - 1))

    level = one(*cuts[0])
    for cut in cuts[1:]:
        level = level * one(*cut)
    return level


def bell_draw(rng, extent, scale, reach, cuts=(), kind=jnp.bfloat16):
    array = jax.random.normal(rng, extent, jnp.float32) * scale
    if len(cuts) > 0:
        array = levels(rng, extent, cuts, -0.22, 0.18) * array
    return jnp.clip(array, min=-reach, max=reach).astype(kind)


def setup_inputs(seed: int = 0) -> dict:
    splits = jax.random.split(jax.random.key(seed), 13)
    return {
        "tokens": bell_draw(splits[0], (IMAGES * PATCHES, D_ENC), 1.0, 6.0, ((0, 128),)),
        "image_slot": draw_image_slot(jax.random.fold_in(splits[12], 71), 0),
        "pairs": draw_pairs(jax.random.fold_in(splits[12], 71), 0),
        "w_embed": bell_draw(splits[3], (D_ENC, D_MODEL), D_ENC ** -0.5, 0.1875),
        "gain_query": jnp.clip(1.0 + 0.18 * jax.random.normal(splits[4], (D_MODEL,), jnp.float32), 0.1, 1.9),
        "gain_key": jnp.clip(1.0 + 0.18 * jax.random.normal(splits[5], (D_MODEL,), jnp.float32), 0.1, 1.9),
        "w_query": bell_draw(splits[6], (D_MODEL, D_MODEL), D_MODEL ** -0.5, 0.21875),
        "w_key": bell_draw(splits[7], (D_MODEL, D_MODEL), D_MODEL ** -0.5, 0.21875),
        "w_value": bell_draw(splits[8], (D_MODEL, D_MODEL), D_MODEL ** -0.5, 0.21875),
        "w_out": bell_draw(splits[9], (D_MODEL, D_MODEL), D_MODEL ** -0.5, 0.21875),
        "gain_head": jnp.clip(1.0 + 0.18 * jax.random.normal(splits[10], (D_MODEL,), jnp.float32), 0.1, 1.9),
        "w_head": bell_draw(splits[11], (D_MODEL, HEAD_OUT), D_MODEL ** -0.5, 0.21875),
    }


def layer_norm(values, gain):
    mean = lax.optimization_barrier(jnp.mean(values, axis=-1, keepdims=True))
    centered = values - mean
    spread = lax.optimization_barrier(jnp.mean(centered * centered, axis=-1, keepdims=True))
    return centered * lax.rsqrt(spread + 1e-06) * gain

def cross_block(queries, keys, gain_query, gain_key, w_query, w_key, w_value, w_out):
    batch, patches, width = queries.shape
    head_dim = width // HEADS
    normed_q = layer_norm(queries.astype(jnp.float32), gain_query).astype(jnp.bfloat16).reshape(batch * patches, width)
    normed_k = layer_norm(keys.astype(jnp.float32), gain_key).astype(jnp.bfloat16).reshape(batch * patches, width)
    query_proj = jnp.dot(normed_q, w_query, preferred_element_type=jnp.float32).astype(jnp.bfloat16)
    key_proj = jnp.dot(normed_k, w_key, preferred_element_type=jnp.float32).astype(jnp.bfloat16)
    value_proj = jnp.dot(normed_k, w_value, preferred_element_type=jnp.float32).astype(jnp.bfloat16)
    query_proj = query_proj.reshape(batch, patches, HEADS, head_dim).astype(jnp.float32)
    key_proj = key_proj.reshape(batch, patches, HEADS, head_dim).astype(jnp.float32)
    value_proj = value_proj.reshape(batch, patches, HEADS, head_dim).astype(jnp.float32)
    scores = jnp.einsum('bqhd,bkhd->bhqk', query_proj, key_proj) * head_dim ** (-0.5)
    expd = jnp.exp(scores)
    weights = (expd / lax.optimization_barrier(jnp.sum(expd, axis=-1, keepdims=True))).astype(jnp.bfloat16)
    attended = jnp.einsum('bhqk,bkhd->bqhd', weights.astype(jnp.float32), value_proj).astype(jnp.bfloat16)
    mixed = jnp.dot(attended.reshape(batch * patches, width), w_out, preferred_element_type=jnp.float32)
    resid = queries.astype(jnp.float32).reshape(batch * patches, width) + mixed
    return resid.astype(jnp.bfloat16).reshape(batch, patches, width)

def point_head(resid, gain_head, w_head):
    batch, patches, width = resid.shape
    normed = layer_norm(resid.astype(jnp.float32), gain_head).astype(jnp.bfloat16).reshape(batch * patches, width)
    raw = jnp.dot(normed, w_head, preferred_element_type=jnp.float32)
    confidence = 1.0 + jnp.exp(raw[:, 3 * PIXELS:])
    weighted = raw[:, :3 * PIXELS] * jnp.tile(confidence, (1, 3))
    joined = jnp.concatenate([weighted, confidence], axis=1).astype(jnp.bfloat16)
    return joined.reshape(batch, patches, 4 * PIXELS)

def reference(tokens, image_slot, pairs, w_embed, gain_query, gain_key, w_query, w_key, w_value, w_out, gain_head, w_head):
    embedded = jnp.dot(tokens, w_embed, preferred_element_type=jnp.float32).astype(jnp.bfloat16)
    embedded = embedded.reshape(IMAGES, PATCHES, D_MODEL)
    slots = image_slot[pairs].astype(jnp.int32)
    first = embedded[slots[:, 0]].reshape(-1, PAIR_DEV, PATCHES, D_MODEL)
    second = embedded[slots[:, 1]].reshape(-1, PAIR_DEV, PATCHES, D_MODEL)

    def one_block(views):
        left, right = views
        queries = jnp.concatenate([left, right], axis=0)
        keys = jnp.concatenate([right, left], axis=0)
        resid = cross_block(queries, keys, gain_query, gain_key, w_query, w_key, w_value, w_out)
        return point_head(resid, gain_head, w_head)
    results = lax.map(one_block, (first, second))
    firsts = results[:, :PAIR_DEV].reshape(PAIRS, PATCHES, HEAD_OUT).astype(jnp.float32)
    seconds = results[:, PAIR_DEV:].reshape(PAIRS, PATCHES, HEAD_OUT).astype(jnp.float32)
    total = jnp.zeros((IMAGES, PATCHES, HEAD_OUT), jnp.float32)
    total = total.at[slots[:, 0]].add(firsts).at[slots[:, 1]].add(seconds)
    return total.reshape(IMAGES * PATCHES, HEAD_OUT)
```

```python
import functools

import jax
import jax.numpy as jnp
from jax import lax
from jax.experimental import pallas as pl
from jax.experimental.pallas import tpu as pltpu
from jax.sharding import PartitionSpec as P

D_ENC = 1024
D_MODEL = 768
HEADS = 12
PATCHES = 196
PIXELS = 256
HEAD_OUT = 1024
IMG_DEV = 8
PAIR_DEV = 8
N_GX = 8
N_GY = 16
SLOTS = 32
SIZES = (48, 48, 48, 52)
PARTS = len(SIZES)
STARTS = tuple(sum(SIZES[:part]) for part in range(PARTS))
PADDED = tuple(-(-size // 16) * 16 for size in SIZES)
ROWS = STARTS[-1] + PADDED[-1]
MESH = pl.DeviceIdType.MESH
BF16 = jnp.bfloat16
F32 = jnp.float32


def ring_distance(step):
    return min(step, 4 - step)


GY_STEPS = sorted(
    [(dx, dy) for dx in range(4) for dy in range(4) if (dx, dy) != (0, 0)],
    key=lambda step: -(ring_distance(step[0]) + ring_distance(step[1])),
)
GX_STEPS = sorted(range(1, N_GX), key=lambda step: -ring_distance(step // 2))


def normalize(values):
    mean = jnp.mean(values, axis=-1, keepdims=True)
    centered = values - mean
    spread = jnp.mean(centered * centered, axis=-1, keepdims=True)
    return centered * lax.rsqrt(spread + 1e-06)


def exchange_kernel(
    image_slot,
    pairs,
    tokens_hbm,
    w_embed_hbm,
    gain_query,
    gain_key,
    w_query_hbm,
    w_key_hbm,
    w_value_hbm,
    w_out_hbm,
    *refs,
):
    back, (table_out,), refs = refs[:PARTS], refs[PARTS : PARTS + 1], refs[PARTS + 1 :]
    send, recv, refs = refs[:PARTS], refs[PARTS : 2 * PARTS], refs[2 * PARTS :]
    (
    tokens,
    w_embed,
    w_query,
    w_key,
    w_value,
    w_out,
    embedded,
    views,
    q_all,
    k_all,
    v_all,
    mixed,
    message,
    got_message,
    lists,
    source,
    inverse,
    load_sem,
    list_sem,
    self_sem,
    msg_send,
    msg_recv,
    fwd_send,
    fwd_recv,
    bwd_send,
    bwd_recv,
    ) = refs
    gx = lax.axis_index("gx")
    gy = lax.axis_index("gy")

    loads = [
        pltpu.make_async_copy(src, dst, load_sem.at[i])
        for i, (src, dst) in enumerate(
            [
                (tokens_hbm, tokens),
                (w_embed_hbm, w_embed),
                (w_query_hbm, w_query),
                (w_key_hbm, w_key),
                (w_value_hbm, w_value),
                (w_out_hbm, w_out),
            ]
        )
    ]
    for load in loads:
        load.start()

    def gy_peer(step):
        dx, dy = step
        return ((gy // 4 + dx) % 4) * 4 + (gy % 4 + dy) % 4

    def gx_peer(step):
        return ((gx // 2 + step // 2) % 4) * 2 + (gx % 2 + step % 2) % 2

    barrier = pltpu.get_barrier_semaphore()
    for step in GY_STEPS:
        pl.semaphore_signal(barrier, inc=1, device_id=(gx, gy_peer(step)), device_id_type=MESH)
    for step in GX_STEPS:
        pl.semaphore_signal(barrier, inc=1, device_id=(gx_peer(step), gy), device_id_type=MESH)

    lane = lax.broadcasted_iota(jnp.int32, (8, 128), 1)
    row = jnp.zeros((8, 128), jnp.int32)
    own = []
    for p in range(PAIR_DEV):
        for s in range(2):
            value = image_slot[pairs[p, s]]
            own.append(value)
            row = jnp.where(lane == 2 * p + s, value, row)
    message[...] = row
    got_message[gy] = row
    got_message[N_GY + gx] = row
    pl.semaphore_wait(barrier, N_GY - 1 + N_GX - 1)

    def message_copy(place, sender, device):
        return pltpu.make_async_remote_copy(
            src_ref=message,
            dst_ref=got_message.at[sender],
            send_sem=msg_send.at[place],
            recv_sem=msg_recv.at[sender],
            device_id=device,
            device_id_type=MESH,
        )

    for step in GY_STEPS:
        peer = gy_peer(step)
        message_copy(peer, gy, (gx, peer)).start()
    for step in GX_STEPS:
        peer = gx_peer(step)
        message_copy(N_GY + peer, N_GY + gx, (peer, gy)).start()

    cols = [(own[2 * p] // IMG_DEV) % N_GY for p in range(PAIR_DEV)]
    rows = [own[2 * p + 1] // (IMG_DEV * N_GY) for p in range(PAIR_DEV)]
    places = []
    for p in range(PAIR_DEV):
        rank = jnp.int32(0)
        for earlier in range(p):
            rank = rank + (rows[earlier] == rows[p]).astype(jnp.int32)
        places.append(N_GY + 2 * rows[p] + rank)
        source[p] = cols[p]
        source[PAIR_DEV + p] = places[p]
    for slot in range(SLOTS):
        view = jnp.int32(0)
        for p in range(PAIR_DEV):
            if slot < N_GY:
                view = jnp.where(cols[p] == slot, p, view)
            else:
                view = jnp.where(places[p] == slot, PAIR_DEV + p, view)
        inverse[slot] = view

    loads[0].wait()
    loads[1].wait()
    half = 4 * PATCHES
    for part in range(2):
        value = jnp.dot(
            tokens[part * half : (part + 1) * half], w_embed[...], preferred_element_type=F32
        )
        for i in range(4):
            embedded[part * 4 + i, :PATCHES] = value[i * PATCHES : (i + 1) * PATCHES].astype(BF16)

    for step in GY_STEPS:
        peer = gy_peer(step)
        copy = message_copy(peer, peer, (gx, peer))
        copy.wait_send()
        copy.wait_recv()
    for step in GX_STEPS:
        peer = gx_peer(step)
        copy = message_copy(N_GY + peer, N_GY + peer, (peer, gy))
        copy.wait_send()
        copy.wait_recv()
    to_lists = pltpu.make_async_copy(got_message, lists, list_sem)
    to_lists.start()
    to_lists.wait()

    def find_first(worker, carry):
        image = jnp.int32(0)
        valid = jnp.int32(0)
        for p in range(PAIR_DEV):
            slot = lists[worker, 0, 2 * p]
            hit = (slot // IMG_DEV) % N_GY == gy
            image = jnp.where(hit, slot % IMG_DEV, image)
            valid = jnp.where(hit, 1, valid)
        table_out[worker] = image
        table_out[SLOTS + worker] = valid
        return carry

    def find_second(worker, carry):
        image = [jnp.int32(0), jnp.int32(0)]
        found = jnp.int32(0)
        for p in range(PAIR_DEV):
            slot = lists[N_GY + worker, 0, 2 * p + 1]
            hit = slot // (IMG_DEV * N_GY) == gx
            for j in range(2):
                image[j] = jnp.where(hit & (found == j), slot % IMG_DEV, image[j])
            found = found + hit.astype(jnp.int32)
        for j in range(2):
            table_out[N_GY + 2 * worker + j] = image[j]
            table_out[SLOTS + N_GY + 2 * worker + j] = jnp.where(found > j, 1, 0)
        return carry

    lax.fori_loop(0, N_GY, find_first, 0)
    lax.fori_loop(0, N_GX, find_second, 0)

    def slot_copies(part, forward):
        target = recv[part] if forward else back[part]
        sent, received = (fwd_send, fwd_recv) if forward else (bwd_send, bwd_recv)

        def gy_copy(peer, sender):
            return pltpu.make_async_remote_copy(
                src_ref=send[part].at[peer],
                dst_ref=target.at[sender],
                send_sem=sent.at[part, peer],
                recv_sem=received.at[part, sender],
                device_id=(gx, peer),
                device_id_type=MESH,
            )

        def gx_copy(peer, sender):
            return pltpu.make_async_remote_copy(
                src_ref=send[part].at[pl.ds(N_GY + 2 * peer, 2)],
                dst_ref=target.at[pl.ds(N_GY + 2 * sender, 2)],
                send_sem=sent.at[part, N_GY + peer],
                recv_sem=received.at[part, N_GY + sender],
                device_id=(peer, gy),
                device_id_type=MESH,
            )

        return gy_copy, gx_copy

    def start_copies(part, forward):
        gy_copy, gx_copy = slot_copies(part, forward)
        for i in range(max(len(GY_STEPS), len(GX_STEPS))):
            gy_copy(gy_peer(GY_STEPS[i]), gy).start()
            if i < len(GX_STEPS):
                gx_copy(gx_peer(GX_STEPS[i]), gx).start()

    def wait_copies(part, forward, what):
        gy_copy, gx_copy = slot_copies(part, forward)

        def wait(copy):
            if what == "send":
                copy.wait_send()
            else:
                copy.wait_recv()

        for step in GY_STEPS:
            peer = gy_peer(step)
            wait(gy_copy(peer, peer))
        for step in GX_STEPS:
            peer = gx_peer(step)
            wait(gx_copy(peer, peer))

    for part in range(PARTS):
        exact = slice(STARTS[part], STARTS[part] + SIZES[part])

        def pack(slot, carry):
            send[part][slot] = embedded[table_out[slot], exact]
            return carry

        lax.fori_loop(0, SLOTS, pack, 0)
        start_copies(part, True)
        for slot in (gy, N_GY + 2 * gx, N_GY + 2 * gx + 1):
            recv[part][slot] = embedded[table_out[slot], exact]
    for load in loads[2:]:
        load.wait()
    views[:, STARTS[-1] :] = jnp.zeros((2 * PAIR_DEV, PADDED[-1], D_MODEL), BF16)

    def project(part):
        wait_copies(part, True, "recv")
        size = PADDED[part]
        exact = slice(STARTS[part], STARTS[part] + SIZES[part])
        place = slice(STARTS[part], STARTS[part] + size)

        def side(group, carry):
            for p in range(PAIR_DEV):
                view = group * PAIR_DEV + p
                views[view, exact] = recv[part][source[view]]
            block = jnp.concatenate(
                [views[group * PAIR_DEV + p, place] for p in range(PAIR_DEV)], axis=0
            ).astype(F32)
            normal = normalize(block)
            normed_q = (normal * gain_query[...]).astype(BF16)
            normed_k = (normal * gain_key[...]).astype(BF16)
            for normed, weight, out, scale in (
                (normed_q, w_query, q_all, (D_MODEL // HEADS) ** -0.5),
                (normed_k, w_key, k_all, None),
                (normed_k, w_value, v_all, None),
            ):
                value = jnp.dot(normed, weight[...], preferred_element_type=F32)
                if scale is not None:
                    value = value * scale
                value = value.astype(BF16)
                for p in range(PAIR_DEV):
                    out[group * PAIR_DEV + p, place] = value[p * size : (p + 1) * size]
            return carry

        lax.fori_loop(0, 2, side, 0)

    for part in range(PARTS):
        project(part)
    for part in range(PARTS):
        wait_copies(part, True, "send")

    def attend(part):
        size = PADDED[part]
        exact = slice(STARTS[part], STARTS[part] + SIZES[part])
        place = slice(STARTS[part], STARTS[part] + size)
        quad = 4 * (D_MODEL // HEADS)
        head_of = lax.broadcasted_iota(jnp.int32, (size, quad), 1) // (D_MODEL // HEADS)
        key_of = lax.broadcasted_iota(jnp.int32, (4 * size, ROWS), 1)

        def one_view(view, carry):
            other = (view + PAIR_DEV) % (2 * PAIR_DEV)
            for four in range(HEADS // 4):
                features = slice(four * quad, (four + 1) * quad)
                query = q_all[view, place, features]
                stacked = jnp.concatenate(
                    [jnp.where(head_of == j, query, jnp.zeros_like(query)) for j in range(4)], axis=0
                )
                scores = lax.dot_general(
                    stacked,
                    k_all[other, :, features],
                    (((1,), (1,)), ((), ())),
                    preferred_element_type=F32,
                )
                scores = jnp.where(key_of < PATCHES, scores, -jnp.inf)
                expd = jnp.exp(scores - jnp.max(scores, axis=-1, keepdims=True))
                weights = (expd * (1.0 / jnp.sum(expd, axis=-1, keepdims=True))).astype(BF16)
                out = jnp.dot(weights, v_all[other, :, features], preferred_element_type=F32)
                attended = out[:size]
                for j in range(1, 4):
                    attended = jnp.where(head_of == j, out[j * size : (j + 1) * size], attended)
                mixed[view, :size, features] = attended.astype(BF16)
            return carry

        lax.fori_loop(0, 2 * PAIR_DEV, one_view, 0)

        def side(group, carry):
            block = jnp.concatenate(
                [mixed[group * PAIR_DEV + p, :size] for p in range(PAIR_DEV)], axis=0
            )
            value = jnp.dot(block, w_out[...], preferred_element_type=F32)
            for p in range(PAIR_DEV):
                view = group * PAIR_DEV + p
                query = views[view, place].astype(F32)
                views[view, place] = (query + value[p * size : (p + 1) * size]).astype(BF16)
            return carry

        lax.fori_loop(0, 2, side, 0)

        def pack(slot, carry):
            send[part][slot] = views[inverse[slot], exact]
            return carry

        lax.fori_loop(0, SLOTS, pack, 0)
        start_copies(part, False)
        for copy in self_copies(part):
            copy.start()

    def self_copies(part):
        return [
            pltpu.make_async_copy(send[part].at[place], back[part].at[place], self_sem.at[part, i])
            for i, place in enumerate([pl.ds(gy, 1), pl.ds(N_GY + 2 * gx, 2)])
        ]

    for part in range(PARTS):
        attend(part)
    for part in range(PARTS):
        for copy in self_copies(part):
            copy.wait()
        wait_copies(part, False, "send")
        wait_copies(part, False, "recv")


def exchange(image_slot, pairs, tokens, w_embed, gain_query, gain_key, w_query, w_key, w_value, w_out):
    any_space = pl.BlockSpec(memory_space=pl.ANY)
    smem = pl.BlockSpec(memory_space=pltpu.SMEM)
    vmem = pl.BlockSpec(memory_space=pltpu.VMEM)
    square = pltpu.VMEM((D_MODEL, D_MODEL), BF16)
    full = pltpu.VMEM((2 * PAIR_DEV, ROWS, D_MODEL), BF16)
    return pl.pallas_call(
        exchange_kernel,
        out_shape=[jax.ShapeDtypeStruct((SLOTS, size, D_MODEL), BF16) for size in SIZES]
        + [jax.ShapeDtypeStruct((2 * SLOTS,), jnp.int32)],
        in_specs=[smem, smem, any_space, any_space, vmem, vmem] + [any_space] * 4,
        out_specs=[any_space] * PARTS + [smem],
        scratch_shapes=[pltpu.VMEM((SLOTS, size, D_MODEL), BF16) for size in SIZES * 2]
        + [
            pltpu.VMEM((IMG_DEV * PATCHES, D_ENC), BF16),
            pltpu.VMEM((D_ENC, D_MODEL), BF16),
            square,
            square,
            square,
            square,
            pltpu.VMEM((IMG_DEV, ROWS, D_MODEL), BF16),
            full,
            full,
            full,
            full,
            pltpu.VMEM((2 * PAIR_DEV, max(PADDED), D_MODEL), BF16),
            pltpu.VMEM((8, 128), jnp.int32),
            pltpu.VMEM((N_GY + N_GX, 8, 128), jnp.int32),
            pltpu.SMEM((N_GY + N_GX, 8, 128), jnp.int32),
            pltpu.SMEM((2 * PAIR_DEV,), jnp.int32),
            pltpu.SMEM((SLOTS,), jnp.int32),
            pltpu.SemaphoreType.DMA((6,)),
            pltpu.SemaphoreType.DMA,
            pltpu.SemaphoreType.DMA((PARTS, 2)),
            pltpu.SemaphoreType.DMA((N_GY + N_GX,)),
            pltpu.SemaphoreType.DMA((N_GY + N_GX,)),
            pltpu.SemaphoreType.DMA((PARTS, N_GY + N_GX)),
            pltpu.SemaphoreType.DMA((PARTS, N_GY + N_GX)),
            pltpu.SemaphoreType.DMA((PARTS, N_GY + N_GX)),
            pltpu.SemaphoreType.DMA((PARTS, N_GY + N_GX)),
        ],
        compiler_params=pltpu.CompilerParams(
            collective_id=0, has_side_effects=True, vmem_limit_bytes=62 * 2**20
        ),
        name="exchange",
    )(image_slot, pairs, tokens, w_embed, gain_query, gain_key, w_query, w_key, w_value, w_out)


def head_kernel(table, *refs):
    sources, (gain, w_head, out), refs = refs[:PARTS], refs[PARTS : PARTS + 3], refs[PARTS + 3 :]
    blocks, (joined, total, order, sems) = refs[:PARTS], refs[PARTS:]

    def collect(slot, count):
        order[count] = slot
        return count + table[SLOTS + slot]

    count = lax.fori_loop(0, SLOTS, collect, jnp.int32(0))

    def copies(item):
        slot = order[item]
        place = item % 2
        return [
            pltpu.make_async_copy(sources[part].at[slot], blocks[part].at[place], sems.at[part, place])
            for part in range(PARTS)
        ]

    @pl.when(count > 0)
    def _():
        for copy in copies(0):
            copy.start()

    total[...] = jnp.zeros_like(total)
    joined[STARTS[-1] :] = jnp.zeros((PADDED[-1], D_MODEL), BF16)

    def step(item, carry):
        @pl.when(item + 1 < count)
        def _():
            for copy in copies(item + 1):
                copy.start()

        for copy in copies(item):
            copy.wait()
        place = item % 2
        image = table[order[item]]
        for start, size, ref in zip(STARTS, SIZES, blocks):
            joined[start : start + size] = ref[place]
        normed = (normalize(joined[...].astype(F32)) * gain[...]).astype(BF16)
        raw = jnp.dot(normed, w_head[...], preferred_element_type=F32)
        confidence = 1.0 + jnp.exp(raw[:, 3 * PIXELS :])
        for plane in range(4):
            columns = slice(plane * PIXELS, (plane + 1) * PIXELS)
            value = confidence if plane == 3 else raw[:, columns] * confidence
            total[image, :, columns] += value.astype(BF16).astype(F32)
        return carry

    lax.fori_loop(0, count, step, 0)
    for image in range(IMG_DEV):
        out[image * PATCHES : (image + 1) * PATCHES] = total[image, :PATCHES]


def head(table, parts, gain, w_head):
    any_space = pl.BlockSpec(memory_space=pl.ANY)
    vmem = pl.BlockSpec(memory_space=pltpu.VMEM)
    return pl.pallas_call(
        head_kernel,
        out_shape=jax.ShapeDtypeStruct((IMG_DEV * PATCHES, HEAD_OUT), F32),
        in_specs=[pl.BlockSpec(memory_space=pltpu.SMEM), *[any_space] * PARTS, vmem, vmem],
        out_specs=vmem,
        scratch_shapes=[pltpu.VMEM((2, size, D_MODEL), BF16) for size in SIZES]
        + [
            pltpu.VMEM((ROWS, D_MODEL), BF16),
            pltpu.VMEM((IMG_DEV, ROWS, HEAD_OUT), F32),
            pltpu.SMEM((SLOTS + 1,), jnp.int32),
            pltpu.SemaphoreType.DMA((PARTS, 2)),
        ],
        compiler_params=pltpu.CompilerParams(vmem_limit_bytes=60 * 2**20),
        name="head",
    )(table, *parts, gain, w_head)


def per_device(
    tokens,
    image_slot,
    pairs,
    w_embed,
    gain_query,
    gain_key,
    w_query,
    w_key,
    w_value,
    w_out,
    gain_head,
    w_head,
):
    *parts, table = exchange(
        image_slot,
        pairs,
        tokens,
        w_embed,
        gain_query.reshape(1, D_MODEL),
        gain_key.reshape(1, D_MODEL),
        w_query,
        w_key,
        w_value,
        w_out,
    )
    return head(table, parts, gain_head.reshape(1, D_MODEL), w_head)


def solution(mesh):
    split = P(("gx", "gy"), None)
    return jax.shard_map(
        per_device,
        mesh=mesh,
        in_specs=(split, P(), split) + (P(),) * 9,
        out_specs=split,
        check_vma=False,
    )
```

```python
import functools

import jax
import jax.numpy as jnp
from jax import lax
from jax.experimental import pallas as pl
from jax.experimental.pallas import tpu as pltpu
from jax.sharding import PartitionSpec as P

D_ENC = 1024
D_MODEL = 768
HEADS = 12
PATCHES = 196
PIXELS = 256
HEAD_OUT = 1024
IMG_DEV = 8
PAIR_DEV = 8
N_GX = 8
N_GY = 16
SLOTS = 32
HEAD_GROUP = 4
GROUP = 4
SIZES = (48, 48, 48, 52)
OUTWARD = (0, 1, 2, 3)
HOMEWARD = (0, 1, 2, 3)
PARTS = len(SIZES)
STARTS = tuple(sum(SIZES[:part]) for part in range(PARTS))
PADDED = tuple(-(-size // 16) * 16 for size in SIZES)
ROWS = STARTS[-1] + PADDED[-1]
MESH = pl.DeviceIdType.MESH
BF16 = jnp.bfloat16
F32 = jnp.float32


def ring_distance(step):
    return min(step, 4 - step)


GY_STEPS = sorted(
    [(dx, dy) for dx in range(4) for dy in range(4) if (dx, dy) != (0, 0)],
    key=lambda step: -(ring_distance(step[0]) + ring_distance(step[1])),
)
GX_STEPS = sorted(range(1, N_GX), key=lambda step: -ring_distance(step // 2))


def normalize(values):
    mean = jnp.mean(values, axis=-1, keepdims=True)
    centered = values - mean
    spread = jnp.mean(centered * centered, axis=-1, keepdims=True)
    return centered * lax.rsqrt(spread + 1e-06)


def exchange_kernel(
    image_slot,
    pairs,
    tokens_hbm,
    w_embed_hbm,
    gain_query,
    gain_key,
    gain_head,
    w_query_hbm,
    w_key_hbm,
    w_value_hbm,
    w_out_hbm,
    *refs,
):
    back, (table_out,), refs = refs[:PARTS], refs[PARTS : PARTS + 1], refs[PARTS + 1 :]
    send, recv, refs = refs[:PARTS], refs[PARTS : 2 * PARTS], refs[2 * PARTS :]
    (
    tokens,
    w_embed,
    w_query,
    w_key,
    w_value,
    w_out,
    embedded,
    views,
    q_all,
    k_all,
    v_all,
    mixed,
    message,
    got_message,
    lists,
    source,
    asks,
    load_sem,
    list_sem,
    self_sem,
    msg_send,
    msg_recv,
    fwd_send,
    fwd_recv,
    bwd_send,
    bwd_recv,
    ) = refs
    gx = lax.axis_index("gx")
    gy = lax.axis_index("gy")

    loads = [
        pltpu.make_async_copy(src, dst, load_sem.at[i])
        for i, (src, dst) in enumerate(
            [
                (tokens_hbm, tokens),
                (w_embed_hbm, w_embed),
                (w_query_hbm, w_query),
                (w_key_hbm, w_key),
                (w_value_hbm, w_value),
                (w_out_hbm, w_out),
            ]
        )
    ]
    for load in loads:
        load.start()

    def gy_peer(step):
        dx, dy = step
        return ((gy // 4 + dx) % 4) * 4 + (gy % 4 + dy) % 4

    def gx_peer(step):
        return ((gx // 2 + step // 2) % 4) * 2 + (gx % 2 + step % 2) % 2

    barrier = pltpu.get_barrier_semaphore()
    for step in GY_STEPS:
        pl.semaphore_signal(barrier, inc=1, device_id=(gx, gy_peer(step)), device_id_type=MESH)
    for step in GX_STEPS:
        pl.semaphore_signal(barrier, inc=1, device_id=(gx_peer(step), gy), device_id_type=MESH)

    lane = lax.broadcasted_iota(jnp.int32, (1, 128), 1)
    asked = jnp.zeros((1, 128), jnp.int32)
    inverse = jnp.zeros((1, 128), jnp.int32)
    rows = []
    for p in range(PAIR_DEV):
        first = image_slot[pairs[0, p]]
        second = image_slot[pairs[1, p]]
        row = second // (IMG_DEV * N_GY)
        rank = jnp.int32(0)
        for earlier in rows:
            rank = rank + jnp.where(earlier == row, 1, 0)
        rows.append(row)
        for view, slot, value in (
            (p, (first // IMG_DEV) % N_GY, first),
            (PAIR_DEV + p, N_GY + 2 * row + rank, second),
        ):
            source[view] = slot
            asked = jnp.where(lane == slot, IMG_DEV + value % IMG_DEV, asked)
            inverse = jnp.where(lane == slot, view, inverse)
    message[...] = asked
    got_message[gy] = asked
    got_message[N_GY + gx] = asked
    got_message[N_GY + N_GX] = inverse
    pl.semaphore_wait(barrier, N_GY - 1 + N_GX - 1)

    def message_copy(place, sender, device):
        return pltpu.make_async_remote_copy(
            src_ref=message,
            dst_ref=got_message.at[sender],
            send_sem=msg_send.at[place],
            recv_sem=msg_recv.at[sender],
            device_id=device,
            device_id_type=MESH,
        )

    for step in GY_STEPS:
        peer = gy_peer(step)
        message_copy(peer, gy, (gx, peer)).start()
    for step in GX_STEPS:
        peer = gx_peer(step)
        message_copy(N_GY + peer, N_GY + gx, (peer, gy)).start()

    loads[0].wait()
    loads[1].wait()
    half = 4 * PATCHES
    for part in range(2):
        value = jnp.dot(
            tokens[part * half : (part + 1) * half], w_embed[...], preferred_element_type=F32
        )
        for i in range(4):
            embedded[part * 4 + i, :PATCHES] = value[i * PATCHES : (i + 1) * PATCHES].astype(BF16)

    for step in GY_STEPS:
        peer = gy_peer(step)
        copy = message_copy(peer, peer, (gx, peer))
        copy.wait_send()
        copy.wait_recv()
    for step in GX_STEPS:
        peer = gx_peer(step)
        copy = message_copy(N_GY + peer, N_GY + peer, (peer, gy))
        copy.wait_send()
        copy.wait_recv()
    to_lists = pltpu.make_async_copy(got_message, lists, list_sem)
    to_lists.start()
    to_lists.wait()

    for slot in range(SLOTS):
        if slot < N_GY:
            value = lists[slot, 0, gy]
        else:
            value = lists[N_GY + (slot - N_GY) // 2, 0, N_GY + 2 * gx + slot % 2]
        asks[slot] = value % IMG_DEV
        table_out[slot] = value

    def slot_copies(part, forward):
        target = recv[part] if forward else back[part]
        sent, received = (fwd_send, fwd_recv) if forward else (bwd_send, bwd_recv)

        def gy_copy(peer, sender):
            return pltpu.make_async_remote_copy(
                src_ref=send[part].at[peer],
                dst_ref=target.at[sender],
                send_sem=sent.at[part, peer],
                recv_sem=received.at[part, sender],
                device_id=(gx, peer),
                device_id_type=MESH,
            )

        def gx_copy(peer, sender):
            return pltpu.make_async_remote_copy(
                src_ref=send[part].at[pl.ds(N_GY + 2 * peer, 2)],
                dst_ref=target.at[pl.ds(N_GY + 2 * sender, 2)],
                send_sem=sent.at[part, N_GY + peer],
                recv_sem=received.at[part, N_GY + sender],
                device_id=(peer, gy),
                device_id_type=MESH,
            )

        return gy_copy, gx_copy

    def start_copies(part, forward):
        gy_copy, gx_copy = slot_copies(part, forward)
        for i in range(max(len(GY_STEPS), len(GX_STEPS))):
            gy_copy(gy_peer(GY_STEPS[i]), gy).start()
            if i < len(GX_STEPS):
                gx_copy(gx_peer(GX_STEPS[i]), gx).start()

    def wait_copies(part, forward, what):
        gy_copy, gx_copy = slot_copies(part, forward)

        def wait(copy):
            if what == "send":
                copy.wait_send()
            else:
                copy.wait_recv()

        for step in GY_STEPS:
            peer = gy_peer(step)
            wait(gy_copy(peer, peer))
        for step in GX_STEPS:
            peer = gx_peer(step)
            wait(gx_copy(peer, peer))

    for part in OUTWARD:
        exact = slice(STARTS[part], STARTS[part] + SIZES[part])

        def pack(slot, carry):
            send[part][slot] = embedded[asks[slot], exact]
            return carry

        lax.fori_loop(0, SLOTS, pack, 0)
        start_copies(part, True)
        for slot in (gy, N_GY + 2 * gx, N_GY + 2 * gx + 1):
            recv[part][slot] = embedded[asks[slot], exact]
    for load in loads[2:]:
        load.wait()
    views[:, STARTS[-1] :] = jnp.zeros((2 * PAIR_DEV, PADDED[-1], D_MODEL), BF16)

    def project(part):
        wait_copies(part, True, "recv")
        size = PADDED[part]
        exact = slice(STARTS[part], STARTS[part] + SIZES[part])
        place = slice(STARTS[part], STARTS[part] + size)

        def side(group, carry):
            for p in range(PAIR_DEV):
                view = group * PAIR_DEV + p
                views[view, exact] = recv[part][source[view]]
            block = jnp.concatenate(
                [views[group * PAIR_DEV + p, place] for p in range(PAIR_DEV)], axis=0
            ).astype(F32)
            normal = normalize(block)
            normed_q = (normal * gain_query[...]).astype(BF16)
            normed_k = (normal * gain_key[...]).astype(BF16)
            for normed, weight, out, scale in (
                (normed_q, w_query, q_all, (D_MODEL // HEADS) ** -0.5),
                (normed_k, w_key, k_all, None),
                (normed_k, w_value, v_all, None),
            ):
                value = jnp.dot(normed, weight[...], preferred_element_type=F32)
                if scale is not None:
                    value = value * scale
                value = value.astype(BF16)
                for p in range(PAIR_DEV):
                    out[group * PAIR_DEV + p, place] = value[p * size : (p + 1) * size]
            return carry

        lax.fori_loop(0, 2, side, 0)

    for part in OUTWARD:
        project(part)
    for part in range(PARTS):
        wait_copies(part, True, "send")

    def attend(part):
        size = PADDED[part]
        exact = slice(STARTS[part], STARTS[part] + SIZES[part])
        place = slice(STARTS[part], STARTS[part] + size)
        quad = 4 * (D_MODEL // HEADS)
        head_of = lax.broadcasted_iota(jnp.int32, (size, quad), 1) // (D_MODEL // HEADS)
        key_of = lax.broadcasted_iota(jnp.int32, (4 * size, ROWS), 1)

        def score(view, features):
            query = q_all[view, place, features]
            stacked = jnp.concatenate(
                [jnp.where(head_of == j, query, jnp.zeros_like(query)) for j in range(4)], axis=0
            )
            return lax.dot_general(
                stacked,
                k_all[(view + PAIR_DEV) % (2 * PAIR_DEV), :, features],
                (((1,), (1,)), ((), ())),
                preferred_element_type=F32,
            )

        def soften(scores):
            scores = jnp.where(key_of < PATCHES, scores, -jnp.inf)
            expd = jnp.exp(scores - jnp.max(scores, axis=-1, keepdims=True))
            return (expd * (1.0 / jnp.sum(expd, axis=-1, keepdims=True))).astype(BF16)

        def gather(view, features, weights):
            out = jnp.dot(
                weights,
                v_all[(view + PAIR_DEV) % (2 * PAIR_DEV), :, features],
                preferred_element_type=F32,
            )
            attended = out[:size]
            for j in range(1, 4):
                attended = jnp.where(head_of == j, out[j * size : (j + 1) * size], attended)
            mixed[view, :size, features] = attended.astype(BF16)

        def some_views(group, carry):
            items = [
                (group * GROUP + i, slice(four * quad, (four + 1) * quad))
                for i in range(GROUP)
                for four in range(HEADS // 4)
            ]
            weights = [soften(scores) for scores in [score(*item) for item in items]]
            for item, weight in zip(items, weights):
                gather(*item, weight)
            return carry

        lax.fori_loop(0, 2 * PAIR_DEV // GROUP, some_views, 0)

        def side(group, carry):
            block = jnp.concatenate(
                [mixed[group * PAIR_DEV + p, :size] for p in range(PAIR_DEV)], axis=0
            )
            value = jnp.dot(block, w_out[...], preferred_element_type=F32)
            for p in range(PAIR_DEV):
                view = group * PAIR_DEV + p
                query = views[view, place].astype(F32)
                resid = (query + value[p * size : (p + 1) * size]).astype(BF16)
                views[view, place] = (normalize(resid.astype(F32)) * gain_head[...]).astype(BF16)
            return carry

        lax.fori_loop(0, 2, side, 0)

        def pack(slot, carry):
            send[part][slot] = views[lists[N_GY + N_GX, 0, slot], exact]
            return carry

        lax.fori_loop(0, SLOTS, pack, 0)
        start_copies(part, False)
        for copy in self_copies(part):
            copy.start()

    def self_copies(part):
        return [
            pltpu.make_async_copy(send[part].at[place], back[part].at[place], self_sem.at[part, i])
            for i, place in enumerate([pl.ds(gy, 1), pl.ds(N_GY + 2 * gx, 2)])
        ]

    for part in HOMEWARD:
        attend(part)
    for part in range(PARTS):
        for copy in self_copies(part):
            copy.wait()
        wait_copies(part, False, "send")
        wait_copies(part, False, "recv")


def exchange(
    image_slot, pairs, tokens, w_embed, gain_query, gain_key, gain_head, w_query, w_key, w_value, w_out
):
    any_space = pl.BlockSpec(memory_space=pl.ANY)
    smem = pl.BlockSpec(memory_space=pltpu.SMEM)
    vmem = pl.BlockSpec(memory_space=pltpu.VMEM)
    square = pltpu.VMEM((D_MODEL, D_MODEL), BF16)
    full = pltpu.VMEM((2 * PAIR_DEV, ROWS, D_MODEL), BF16)
    return pl.pallas_call(
        exchange_kernel,
        out_shape=[jax.ShapeDtypeStruct((SLOTS, size, D_MODEL), BF16) for size in SIZES]
        + [jax.ShapeDtypeStruct((SLOTS,), jnp.int32)],
        in_specs=[smem, smem, any_space, any_space, vmem, vmem, vmem] + [any_space] * 4,
        out_specs=[any_space] * PARTS + [smem],
        scratch_shapes=[pltpu.VMEM((SLOTS, size, D_MODEL), BF16) for size in SIZES * 2]
        + [
            pltpu.VMEM((IMG_DEV * PATCHES, D_ENC), BF16),
            pltpu.VMEM((D_ENC, D_MODEL), BF16),
            square,
            square,
            square,
            square,
            pltpu.VMEM((IMG_DEV, ROWS, D_MODEL), BF16),
            full,
            full,
            full,
            full,
            pltpu.VMEM((2 * PAIR_DEV, max(PADDED), D_MODEL), BF16),
            pltpu.VMEM((1, 128), jnp.int32),
            pltpu.VMEM((N_GY + N_GX + 1, 1, 128), jnp.int32),
            pltpu.SMEM((N_GY + N_GX + 1, 1, 128), jnp.int32),
            pltpu.SMEM((2 * PAIR_DEV,), jnp.int32),
            pltpu.SMEM((SLOTS,), jnp.int32),
            pltpu.SemaphoreType.DMA((6,)),
            pltpu.SemaphoreType.DMA,
            pltpu.SemaphoreType.DMA((PARTS, 2)),
            pltpu.SemaphoreType.DMA((N_GY + N_GX,)),
            pltpu.SemaphoreType.DMA((N_GY + N_GX,)),
            pltpu.SemaphoreType.DMA((PARTS, N_GY + N_GX)),
            pltpu.SemaphoreType.DMA((PARTS, N_GY + N_GX)),
            pltpu.SemaphoreType.DMA((PARTS, N_GY + N_GX)),
            pltpu.SemaphoreType.DMA((PARTS, N_GY + N_GX)),
        ],
        compiler_params=pltpu.CompilerParams(
            collective_id=0, has_side_effects=True, vmem_limit_bytes=62 * 2**20
        ),
        name="exchange",
    )(image_slot, pairs, tokens, w_embed, gain_query, gain_key, gain_head, w_query, w_key, w_value, w_out)


def head_kernel(table, *refs):
    sources, (w_head, out), refs = refs[:PARTS], refs[PARTS : PARTS + 2], refs[PARTS + 2 :]
    blocks, (joined, total, order, sems) = refs[:PARTS], refs[PARTS:]

    def collect(slot, count):
        order[count] = slot
        return count + jnp.where(table[slot] >= IMG_DEV, 1, 0)

    count = lax.fori_loop(0, SLOTS, collect, jnp.int32(0))

    for i in range(HEAD_GROUP - 1):
        order[count + i] = SLOTS
    steps = (count + HEAD_GROUP - 1) // HEAD_GROUP

    def copies(step):
        for i in range(HEAD_GROUP):
            slot = order[step * HEAD_GROUP + i] % SLOTS
            place = (step % 2) * HEAD_GROUP + i
            for part in range(PARTS):
                yield pltpu.make_async_copy(
                    sources[part].at[slot], blocks[part].at[place], sems.at[part, place]
                )

    @pl.when(steps > 0)
    def _():
        for copy in copies(0):
            copy.start()

    total[...] = jnp.zeros_like(total)
    for i in range(HEAD_GROUP):
        joined[i, STARTS[-1] :] = jnp.zeros((PADDED[-1], D_MODEL), BF16)

    def one_step(step, carry):
        @pl.when(step + 1 < steps)
        def _():
            for copy in copies(step + 1):
                copy.start()

        for copy in copies(step):
            copy.wait()
        raws = []
        for i in range(HEAD_GROUP):
            for start, size, ref in zip(STARTS, SIZES, blocks):
                joined[i, start : start + size] = ref[(step % 2) * HEAD_GROUP + i]
            raws.append(jnp.dot(joined[i], w_head[...], preferred_element_type=F32))
        for i in range(HEAD_GROUP):
            slot = order[step * HEAD_GROUP + i]
            image = jnp.where(slot < SLOTS, table[slot % SLOTS] % IMG_DEV, IMG_DEV)
            confidence = 1.0 + jnp.exp(raws[i][:, 3 * PIXELS :])
            for plane in range(4):
                columns = slice(plane * PIXELS, (plane + 1) * PIXELS)
                value = confidence if plane == 3 else raws[i][:, columns] * confidence
                total[image, :, columns] += value.astype(BF16).astype(F32)
        return carry

    lax.fori_loop(0, steps, one_step, 0)
    for image in range(IMG_DEV):
        out[image * PATCHES : (image + 1) * PATCHES] = total[image, :PATCHES]


def head(table, parts, w_head):
    any_space = pl.BlockSpec(memory_space=pl.ANY)
    vmem = pl.BlockSpec(memory_space=pltpu.VMEM)
    return pl.pallas_call(
        head_kernel,
        out_shape=jax.ShapeDtypeStruct((IMG_DEV * PATCHES, HEAD_OUT), F32),
        in_specs=[pl.BlockSpec(memory_space=pltpu.SMEM), *[any_space] * PARTS, vmem],
        out_specs=vmem,
        scratch_shapes=[pltpu.VMEM((2 * HEAD_GROUP, size, D_MODEL), BF16) for size in SIZES]
        + [
            pltpu.VMEM((HEAD_GROUP, ROWS, D_MODEL), BF16),
            pltpu.VMEM((IMG_DEV + 1, ROWS, HEAD_OUT), F32),
            pltpu.SMEM((SLOTS + HEAD_GROUP,), jnp.int32),
            pltpu.SemaphoreType.DMA((PARTS, 2 * HEAD_GROUP)),
        ],
        compiler_params=pltpu.CompilerParams(vmem_limit_bytes=60 * 2**20),
        name="head",
    )(table, *parts, w_head)


def per_device(
    tokens,
    image_slot,
    pairs,
    w_embed,
    gain_query,
    gain_key,
    w_query,
    w_key,
    w_value,
    w_out,
    gain_head,
    w_head,
):
    *parts, table = exchange(
        image_slot,
        pairs.T,
        tokens,
        w_embed,
        gain_query,
        gain_key,
        gain_head,
        w_query,
        w_key,
        w_value,
        w_out,
    )
    return head(table, parts, w_head)


def solution(mesh):
    split = P(("gx", "gy"), None)
    return jax.shard_map(
        per_device,
        mesh=mesh,
        in_specs=(split, P(), split) + (P(),) * 9,
        out_specs=split,
        check_vma=False,
    )
```

```python
import functools

import jax
import jax.numpy as jnp
from jax import lax
from jax.experimental import pallas as pl
from jax.experimental.pallas import tpu as pltpu
from jax.sharding import PartitionSpec as P

D_ENC = 1024
D_MODEL = 768
HEADS = 12
PATCHES = 196
PIXELS = 256
HEAD_OUT = 1024
IMG_DEV = 8
PAIR_DEV = 8
N_GX = 8
N_GY = 16
SLOTS = 32
COUPLES = IMG_DEV // 2
DEPTH = 6
GROUP = 4
SIZES = (16, 48, 48, 48, 36)
OUTWARD = (1, 2, 3, 4, 0)
HOMEWARD = (1, 2, 3, 4, 0)
PARTS = len(SIZES)
STARTS = tuple(sum(SIZES[:part]) for part in range(PARTS))
PADDED = tuple(-(-size // 16) * 16 for size in SIZES)
LAST = HOMEWARD[-1]
ROWS = STARTS[-1] + PADDED[-1]
MESH = pl.DeviceIdType.MESH
BF16 = jnp.bfloat16
F32 = jnp.float32


def ring_distance(step):
    return min(step, 4 - step)


GY_STEPS = sorted(
    [(dx, dy) for dx in range(4) for dy in range(4) if (dx, dy) != (0, 0)],
    key=lambda step: -(ring_distance(step[0]) + ring_distance(step[1])),
)
GX_STEPS = sorted(range(1, N_GX), key=lambda step: -ring_distance(step // 2))


def normalize(values):
    mean = jnp.mean(values, axis=-1, keepdims=True)
    centered = values - mean
    spread = jnp.mean(centered * centered, axis=-1, keepdims=True)
    return centered * lax.rsqrt(spread + 1e-06)


def exchange_kernel(
    image_slot,
    pairs,
    tokens_hbm,
    w_embed_hbm,
    gain_query,
    gain_key,
    gain_head,
    w_query_hbm,
    w_key_hbm,
    w_value_hbm,
    w_out_hbm,
    w_head_hbm,
    *refs,
):
    given, table_out, *refs = refs
    back, refs = list(refs[: PARTS - 1]), refs[PARTS - 1 :]
    send, recv, refs = refs[:PARTS], refs[PARTS : 2 * PARTS], refs[2 * PARTS :]
    (
    tokens,
    w_embed,
    w_query,
    w_key,
    w_value,
    w_out,
    w_head,
    last_back,
    offered,
    embedded,
    views,
    q_all,
    k_all,
    v_all,
    mixed,
    message,
    got_message,
    lists,
    source,
    asks,
    load_sem,
    list_sem,
    self_sem,
    head_sem,
    msg_send,
    msg_recv,
    fwd_send,
    fwd_recv,
    bwd_send,
    bwd_recv,
    ) = refs
    gx = lax.axis_index("gx")
    gy = lax.axis_index("gy")
    back.insert(LAST, last_back)

    loads = [
        pltpu.make_async_copy(src, dst, load_sem.at[i])
        for i, (src, dst) in enumerate(
            [
                (tokens_hbm, tokens),
                (w_embed_hbm, w_embed),
                (w_query_hbm, w_query),
                (w_key_hbm, w_key),
                (w_value_hbm, w_value),
                (w_out_hbm, w_out),
                (w_head_hbm, w_head),
            ]
        )
    ]
    for load in loads:
        load.start()

    def gy_peer(step):
        dx, dy = step
        return ((gy // 4 + dx) % 4) * 4 + (gy % 4 + dy) % 4

    def gx_peer(step):
        return ((gx // 2 + step // 2) % 4) * 2 + (gx % 2 + step % 2) % 2

    barrier = pltpu.get_barrier_semaphore()
    for step in GY_STEPS:
        pl.semaphore_signal(barrier, inc=1, device_id=(gx, gy_peer(step)), device_id_type=MESH)
    for step in GX_STEPS:
        pl.semaphore_signal(barrier, inc=1, device_id=(gx_peer(step), gy), device_id_type=MESH)

    lane = lax.broadcasted_iota(jnp.int32, (1, 128), 1)
    asked = jnp.zeros((1, 128), jnp.int32)
    inverse = jnp.zeros((1, 128), jnp.int32)
    rows = []
    for p in range(PAIR_DEV):
        first = image_slot[pairs[0, p]]
        second = image_slot[pairs[1, p]]
        row = second // (IMG_DEV * N_GY)
        rank = jnp.int32(0)
        for earlier in rows:
            rank = rank + jnp.where(earlier == row, 1, 0)
        rows.append(row)
        for view, slot, value in (
            (p, (first // IMG_DEV) % N_GY, first),
            (PAIR_DEV + p, N_GY + 2 * row + rank, second),
        ):
            source[view] = slot
            asked = jnp.where(lane == slot, IMG_DEV + value % IMG_DEV, asked)
            inverse = jnp.where(lane == slot, view, inverse)
    message[...] = asked
    got_message[gy] = asked
    got_message[N_GY + gx] = asked
    got_message[N_GY + N_GX] = inverse
    pl.semaphore_wait(barrier, N_GY - 1 + N_GX - 1)

    def message_copy(place, sender, device):
        return pltpu.make_async_remote_copy(
            src_ref=message,
            dst_ref=got_message.at[sender],
            send_sem=msg_send.at[place],
            recv_sem=msg_recv.at[sender],
            device_id=device,
            device_id_type=MESH,
        )

    for step in GY_STEPS:
        peer = gy_peer(step)
        message_copy(peer, gy, (gx, peer)).start()
    for step in GX_STEPS:
        peer = gx_peer(step)
        message_copy(N_GY + peer, N_GY + gx, (peer, gy)).start()

    loads[0].wait()
    loads[1].wait()
    half = 4 * PATCHES
    for part in range(2):
        value = jnp.dot(
            tokens[part * half : (part + 1) * half], w_embed[...], preferred_element_type=F32
        )
        for i in range(4):
            embedded[part * 4 + i, :PATCHES] = value[i * PATCHES : (i + 1) * PATCHES].astype(BF16)

    for step in GY_STEPS:
        peer = gy_peer(step)
        copy = message_copy(peer, peer, (gx, peer))
        copy.wait_send()
        copy.wait_recv()
    for step in GX_STEPS:
        peer = gx_peer(step)
        copy = message_copy(N_GY + peer, N_GY + peer, (peer, gy))
        copy.wait_send()
        copy.wait_recv()
    to_lists = pltpu.make_async_copy(got_message, lists, list_sem)
    to_lists.start()
    to_lists.wait()

    for slot in range(SLOTS):
        if slot < N_GY:
            value = lists[slot, 0, gy]
        else:
            value = lists[N_GY + (slot - N_GY) // 2, 0, N_GY + 2 * gx + slot % 2]
        asks[slot] = value % IMG_DEV
        table_out[slot] = value

    def slot_copies(part, forward):
        target = recv[part] if forward else back[part]
        sent, received = (fwd_send, fwd_recv) if forward else (bwd_send, bwd_recv)

        def gy_copy(peer, sender):
            return pltpu.make_async_remote_copy(
                src_ref=send[part].at[peer],
                dst_ref=target.at[sender],
                send_sem=sent.at[part, peer],
                recv_sem=received.at[part, sender],
                device_id=(gx, peer),
                device_id_type=MESH,
            )

        def gx_copy(peer, sender):
            return pltpu.make_async_remote_copy(
                src_ref=send[part].at[pl.ds(N_GY + 2 * peer, 2)],
                dst_ref=target.at[pl.ds(N_GY + 2 * sender, 2)],
                send_sem=sent.at[part, N_GY + peer],
                recv_sem=received.at[part, N_GY + sender],
                device_id=(peer, gy),
                device_id_type=MESH,
            )

        return gy_copy, gx_copy

    def start_copies(part, forward):
        gy_copy, gx_copy = slot_copies(part, forward)
        for i in range(max(len(GY_STEPS), len(GX_STEPS))):
            gy_copy(gy_peer(GY_STEPS[i]), gy).start()
            if i < len(GX_STEPS):
                gx_copy(gx_peer(GX_STEPS[i]), gx).start()

    def wait_copies(part, forward, what):
        gy_copy, gx_copy = slot_copies(part, forward)

        def wait(copy):
            if what == "send":
                copy.wait_send()
            else:
                copy.wait_recv()

        for step in GY_STEPS:
            peer = gy_peer(step)
            wait(gy_copy(peer, peer))
        for step in GX_STEPS:
            peer = gx_peer(step)
            wait(gx_copy(peer, peer))

    for part in OUTWARD:
        exact = slice(STARTS[part], STARTS[part] + SIZES[part])

        def pack(slot, carry):
            send[part][slot] = embedded[asks[slot], exact]
            return carry

        lax.fori_loop(0, SLOTS, pack, 0)
        start_copies(part, True)
        for slot in (gy, N_GY + 2 * gx, N_GY + 2 * gx + 1):
            recv[part][slot] = embedded[asks[slot], exact]
    for load in loads[2:]:
        load.wait()
    views[:, STARTS[-1] :] = jnp.zeros((2 * PAIR_DEV, PADDED[-1], D_MODEL), BF16)

    def project(part):
        wait_copies(part, True, "recv")
        size = PADDED[part]
        exact = slice(STARTS[part], STARTS[part] + SIZES[part])
        place = slice(STARTS[part], STARTS[part] + size)

        def side(group, carry):
            for p in range(PAIR_DEV):
                view = group * PAIR_DEV + p
                views[view, exact] = recv[part][source[view]]
            block = jnp.concatenate(
                [views[group * PAIR_DEV + p, place] for p in range(PAIR_DEV)], axis=0
            ).astype(F32)
            normal = normalize(block)
            normed_q = (normal * gain_query[...]).astype(BF16)
            normed_k = (normal * gain_key[...]).astype(BF16)
            for normed, weight, out, scale in (
                (normed_q, w_query, q_all, (D_MODEL // HEADS) ** -0.5),
                (normed_k, w_key, k_all, None),
                (normed_k, w_value, v_all, None),
            ):
                value = jnp.dot(normed, weight[...], preferred_element_type=F32)
                if scale is not None:
                    value = value * scale
                value = value.astype(BF16)
                for p in range(PAIR_DEV):
                    out[group * PAIR_DEV + p, place] = value[p * size : (p + 1) * size]
            return carry

        lax.fori_loop(0, 2, side, 0)

    for part in OUTWARD:
        project(part)
    for part in range(PARTS):
        wait_copies(part, True, "send")

    def attend(part):
        size = PADDED[part]
        exact = slice(STARTS[part], STARTS[part] + SIZES[part])
        place = slice(STARTS[part], STARTS[part] + size)
        quad = 4 * (D_MODEL // HEADS)
        head_of = lax.broadcasted_iota(jnp.int32, (size, quad), 1) // (D_MODEL // HEADS)
        key_of = lax.broadcasted_iota(jnp.int32, (4 * size, ROWS), 1)
        at_once = 2 * GROUP if size <= 16 else GROUP

        def score(view, features):
            query = q_all[view, place, features]
            stacked = jnp.concatenate(
                [jnp.where(head_of == j, query, jnp.zeros_like(query)) for j in range(4)], axis=0
            )
            return lax.dot_general(
                stacked,
                k_all[(view + PAIR_DEV) % (2 * PAIR_DEV), :, features],
                (((1,), (1,)), ((), ())),
                preferred_element_type=F32,
            )

        def soften(scores):
            scores = jnp.where(key_of < PATCHES, scores, -jnp.inf)
            expd = jnp.exp(scores - jnp.max(scores, axis=-1, keepdims=True))
            return (expd * (1.0 / jnp.sum(expd, axis=-1, keepdims=True))).astype(BF16)

        def gather(view, features, weights):
            out = jnp.dot(
                weights,
                v_all[(view + PAIR_DEV) % (2 * PAIR_DEV), :, features],
                preferred_element_type=F32,
            )
            attended = out[:size]
            for j in range(1, 4):
                attended = jnp.where(head_of == j, out[j * size : (j + 1) * size], attended)
            mixed[view, :size, features] = attended.astype(BF16)

        def some_views(group, carry):
            items = [
                (group * at_once + i, slice(four * quad, (four + 1) * quad))
                for i in range(at_once)
                for four in range(HEADS // 4)
            ]
            weights = [soften(scores) for scores in [score(*item) for item in items]]
            for item, weight in zip(items, weights):
                gather(*item, weight)
            return carry

        lax.fori_loop(0, 2 * PAIR_DEV // at_once, some_views, 0)

        def side(group, carry):
            block = jnp.concatenate(
                [mixed[group * PAIR_DEV + p, :size] for p in range(PAIR_DEV)], axis=0
            )
            value = jnp.dot(block, w_out[...], preferred_element_type=F32)
            for p in range(PAIR_DEV):
                view = group * PAIR_DEV + p
                query = views[view, place].astype(F32)
                resid = (query + value[p * size : (p + 1) * size]).astype(BF16)
                views[view, place] = (normalize(resid.astype(F32)) * gain_head[...]).astype(BF16)
            return carry

        lax.fori_loop(0, 2, side, 0)

        def pack(slot, carry):
            send[part][slot] = views[lists[N_GY + N_GX, 0, slot], exact]
            return carry

        lax.fori_loop(0, SLOTS, pack, 0)
        start_copies(part, False)
        for copy in self_copies(part):
            copy.start()

    def self_copies(part):
        return [
            pltpu.make_async_copy(send[part].at[place], back[part].at[place], self_sem.at[part, i])
            for i, place in enumerate([pl.ds(gy, 1), pl.ds(N_GY + 2 * gx, 2)])
        ]

    for part in HOMEWARD:
        attend(part)
    def leave(part):
        size = PADDED[part]
        return pltpu.make_async_copy(
            offered.at[:, pl.ds(0, size)],
            given.at[:, pl.ds(STARTS[part], size)],
            head_sem.at[PARTS + part],
        )

    def contribute(part, landed):
        size = PADDED[part]
        exact = slice(STARTS[part], STARTS[part] + SIZES[part])
        place = slice(STARTS[part], STARTS[part] + size)

        def some_slots(group, carry):
            for p in range(PAIR_DEV):
                views[p, exact] = landed[group * PAIR_DEV + p]
            normed = jnp.concatenate([views[p, place] for p in range(PAIR_DEV)], axis=0)
            raw = jnp.dot(normed, w_head[...], preferred_element_type=F32)
            confidence = 1.0 + jnp.exp(raw[:, 3 * PIXELS :])
            for plane in range(4):
                columns = slice(plane * PIXELS, (plane + 1) * PIXELS)
                value = confidence if plane == 3 else raw[:, columns] * confidence
                value = value.astype(BF16)
                for p in range(PAIR_DEV):
                    offered[group * PAIR_DEV + p, :size, columns] = value[p * size : (p + 1) * size]
            return carry

        lax.fori_loop(0, SLOTS // PAIR_DEV, some_slots, 0)

    previous = None
    for part in HOMEWARD:
        for copy in self_copies(part):
            copy.wait()
        wait_copies(part, False, "recv")
        landed = last_back
        if part != LAST:
            landed = recv[part]
            arrive = pltpu.make_async_copy(back[part], landed, head_sem.at[part])
            arrive.start()
            arrive.wait()
        if previous is not None:
            previous.wait()
        contribute(part, landed)
        previous = leave(part)
        previous.start()
    for part in HOMEWARD:
        wait_copies(part, False, "send")
    previous.wait()


def exchange(
    image_slot, pairs, tokens, w_embed, gain_query, gain_key, gain_head, w_query, w_key, w_value, w_out, w_head
):
    any_space = pl.BlockSpec(memory_space=pl.ANY)
    smem = pl.BlockSpec(memory_space=pltpu.SMEM)
    vmem = pl.BlockSpec(memory_space=pltpu.VMEM)
    square = pltpu.VMEM((D_MODEL, D_MODEL), BF16)
    full = pltpu.VMEM((2 * PAIR_DEV, ROWS, D_MODEL), BF16)
    return pl.pallas_call(
        exchange_kernel,
        out_shape=[
            jax.ShapeDtypeStruct((SLOTS, ROWS, HEAD_OUT), BF16),
            jax.ShapeDtypeStruct((SLOTS,), jnp.int32),
        ]
        + [
            jax.ShapeDtypeStruct((SLOTS, size, D_MODEL), BF16)
            for part, size in enumerate(SIZES)
            if part != LAST
        ],
        in_specs=[smem, smem, any_space, any_space, vmem, vmem, vmem] + [any_space] * 5,
        out_specs=[any_space, smem] + [any_space] * (PARTS - 1),
        scratch_shapes=[pltpu.VMEM((SLOTS, size, D_MODEL), BF16) for size in SIZES * 2]
        + [
            pltpu.VMEM((IMG_DEV * PATCHES, D_ENC), BF16),
            pltpu.VMEM((D_ENC, D_MODEL), BF16),
            square,
            square,
            square,
            square,
            pltpu.VMEM((D_MODEL, HEAD_OUT), BF16),
            pltpu.VMEM((SLOTS, SIZES[LAST], D_MODEL), BF16),
            pltpu.VMEM((SLOTS, max(PADDED), HEAD_OUT), BF16),
            pltpu.VMEM((IMG_DEV, ROWS, D_MODEL), BF16),
            full,
            full,
            full,
            full,
            pltpu.VMEM((2 * PAIR_DEV, max(PADDED), D_MODEL), BF16),
            pltpu.VMEM((1, 128), jnp.int32),
            pltpu.VMEM((N_GY + N_GX + 1, 1, 128), jnp.int32),
            pltpu.SMEM((N_GY + N_GX + 1, 1, 128), jnp.int32),
            pltpu.SMEM((2 * PAIR_DEV,), jnp.int32),
            pltpu.SMEM((SLOTS,), jnp.int32),
            pltpu.SemaphoreType.DMA((7,)),
            pltpu.SemaphoreType.DMA,
            pltpu.SemaphoreType.DMA((PARTS, 2)),
            pltpu.SemaphoreType.DMA((2 * PARTS,)),
            pltpu.SemaphoreType.DMA((N_GY + N_GX,)),
            pltpu.SemaphoreType.DMA((N_GY + N_GX,)),
            pltpu.SemaphoreType.DMA((PARTS, N_GY + N_GX)),
            pltpu.SemaphoreType.DMA((PARTS, N_GY + N_GX)),
            pltpu.SemaphoreType.DMA((PARTS, N_GY + N_GX)),
            pltpu.SemaphoreType.DMA((PARTS, N_GY + N_GX)),
        ],
        compiler_params=pltpu.CompilerParams(
            collective_id=0, has_side_effects=True, vmem_limit_bytes=62 * 2**20
        ),
        name="exchange",
    )(image_slot, pairs, tokens, w_embed, gain_query, gain_key, gain_head, w_query, w_key, w_value, w_out, w_head)


def sum_kernel(table, source, out, block, total, staged, first, order, sems, out_sems):
    def place_of(slot):
        return jnp.where(table[slot] >= IMG_DEV, (table[slot] % IMG_DEV) // 2, COUPLES)

    for couple in range(COUPLES + 1):
        first[couple] = 0

    def tally(slot, carry):
        couple = place_of(slot)
        first[couple] = first[couple] + 1
        return carry

    lax.fori_loop(0, SLOTS, tally, 0)
    bounds = [jnp.int32(0)]
    for couple in range(COUPLES):
        bounds.append(bounds[-1] + first[couple])
    for couple in range(COUPLES + 1):
        first[couple] = bounds[couple]

    def arrange(slot, carry):
        couple = place_of(slot)
        order[first[couple]] = slot
        first[couple] = first[couple] + 1
        return carry

    lax.fori_loop(0, SLOTS, arrange, 0)
    count = bounds[-1]

    def copy(item):
        place = item % DEPTH
        return pltpu.make_async_copy(source.at[order[item]], block.at[place], sems.at[place])

    def start(item):
        @pl.when(item < count)
        def _():
            copy(item).start()

    for item in range(DEPTH - 1):
        start(item)
    total[...] = jnp.zeros_like(total)

    def one_item(item, carry):
        start(item + DEPTH - 1)
        copy(item).wait()
        total[table[order[item]] % IMG_DEV] += block[item % DEPTH].astype(F32)
        return carry

    leaving = []
    for couple in range(COUPLES):
        lax.fori_loop(bounds[couple], bounds[couple + 1], one_item, 0)
        for image in (2 * couple, 2 * couple + 1):
            staged[image * PATCHES : (image + 1) * PATCHES] = total[image, :PATCHES]
        rows = slice(2 * couple * PATCHES, 2 * (couple + 1) * PATCHES)
        leaving.append(pltpu.make_async_copy(staged.at[rows], out.at[rows], out_sems.at[couple]))
        leaving[-1].start()
    for parting in leaving:
        parting.wait()


def sum_slots(table, contributions):
    any_space = pl.BlockSpec(memory_space=pl.ANY)
    return pl.pallas_call(
        sum_kernel,
        out_shape=jax.ShapeDtypeStruct((IMG_DEV * PATCHES, HEAD_OUT), F32),
        in_specs=[pl.BlockSpec(memory_space=pltpu.SMEM), any_space],
        out_specs=any_space,
        scratch_shapes=[
            pltpu.VMEM((DEPTH, ROWS, HEAD_OUT), BF16),
            pltpu.VMEM((IMG_DEV, ROWS, HEAD_OUT), F32),
            pltpu.VMEM((IMG_DEV * PATCHES, HEAD_OUT), F32),
            pltpu.SMEM((COUPLES + 1,), jnp.int32),
            pltpu.SMEM((SLOTS,), jnp.int32),
            pltpu.SemaphoreType.DMA((DEPTH,)),
            pltpu.SemaphoreType.DMA((COUPLES,)),
        ],
        compiler_params=pltpu.CompilerParams(vmem_limit_bytes=60 * 2**20),
        name="sum_slots",
    )(table, contributions)


def per_device(
    tokens,
    image_slot,
    pairs,
    w_embed,
    gain_query,
    gain_key,
    w_query,
    w_key,
    w_value,
    w_out,
    gain_head,
    w_head,
):
    contributions, table, *_ = exchange(
        image_slot,
        pairs.T,
        tokens,
        w_embed,
        gain_query,
        gain_key,
        gain_head,
        w_query,
        w_key,
        w_value,
        w_out,
        w_head,
    )
    return sum_slots(table, contributions)


def solution(mesh):
    split = P(("gx", "gy"), None)
    return jax.shard_map(
        per_device,
        mesh=mesh,
        in_specs=(split, P(), split) + (P(),) * 9,
        out_specs=split,
        check_vma=False,
    )
```

```python
import functools

import jax
import jax.numpy as jnp
from jax import lax
from jax.experimental import pallas as pl
from jax.experimental.pallas import tpu as pltpu
from jax.sharding import PartitionSpec as P

D_ENC = 1024
D_MODEL = 768
HEADS = 12
PATCHES = 196
PIXELS = 256
HEAD_OUT = 1024
IMG_DEV = 8
PAIR_DEV = 8
N_GX = 8
N_GY = 16
SLOTS = 32
COUPLES = IMG_DEV // 2
DEPTH = 6
GROUP = 4
SIZES = (16, 48, 48, 48, 36)
OUTWARD = (1, 2, 3, 4, 0)
HOMEWARD = (1, 2, 3, 4, 0)
PARTS = len(SIZES)
STARTS = tuple(sum(SIZES[:part]) for part in range(PARTS))
PADDED = tuple(-(-size // 16) * 16 for size in SIZES)
LAST = HOMEWARD[-1]
ROWS = STARTS[-1] + PADDED[-1]
MESH = pl.DeviceIdType.MESH
BF16 = jnp.bfloat16
F32 = jnp.float32


def ring_distance(step):
    return min(step, 4 - step)


GY_STEPS = sorted(
    [(dx, dy) for dx in range(4) for dy in range(4) if (dx, dy) != (0, 0)],
    key=lambda step: -(ring_distance(step[0]) + ring_distance(step[1])),
)
GX_STEPS = sorted(range(1, N_GX), key=lambda step: -ring_distance(step // 2))


def normalize(values):
    mean = jnp.mean(values, axis=-1, keepdims=True)
    centered = values - mean
    spread = jnp.mean(centered * centered, axis=-1, keepdims=True)
    return centered * lax.rsqrt(spread + 1e-06)


def exchange_kernel(
    image_slot,
    pairs,
    tokens_hbm,
    w_embed_hbm,
    gain_query,
    gain_key,
    gain_head,
    w_query_hbm,
    w_key_hbm,
    w_value_hbm,
    w_out_hbm,
    w_head_hbm,
    *refs,
):
    given, table_out, *refs = refs
    back, refs = list(refs[: PARTS - 1]), refs[PARTS - 1 :]
    send, recv, refs = refs[:PARTS], refs[PARTS : 2 * PARTS], refs[2 * PARTS :]
    (
    tokens,
    w_embed,
    w_query,
    w_key,
    w_value,
    w_out,
    w_head,
    last_back,
    offered,
    embedded,
    views,
    q_all,
    k_all,
    v_all,
    mixed,
    message,
    got_message,
    lists,
    source,
    asks,
    load_sem,
    list_sem,
    self_sem,
    head_sem,
    msg_send,
    msg_recv,
    fwd_send,
    fwd_recv,
    bwd_send,
    bwd_recv,
    ) = refs
    gx = lax.axis_index("gx")
    gy = lax.axis_index("gy")
    back.insert(LAST, last_back)

    loads = [
        pltpu.make_async_copy(src, dst, load_sem.at[i])
        for i, (src, dst) in enumerate(
            [
                (tokens_hbm, tokens),
                (w_embed_hbm, w_embed),
                (w_query_hbm, w_query),
                (w_key_hbm, w_key),
                (w_value_hbm, w_value),
                (w_out_hbm, w_out),
                (w_head_hbm, w_head),
            ]
        )
    ]
    for load in loads:
        load.start()

    def gy_peer(step):
        dx, dy = step
        return ((gy // 4 + dx) % 4) * 4 + (gy % 4 + dy) % 4

    def gx_peer(step):
        return ((gx // 2 + step // 2) % 4) * 2 + (gx % 2 + step % 2) % 2

    barrier = pltpu.get_barrier_semaphore()
    for step in GY_STEPS:
        pl.semaphore_signal(barrier, inc=1, device_id=(gx, gy_peer(step)), device_id_type=MESH)
    for step in GX_STEPS:
        pl.semaphore_signal(barrier, inc=1, device_id=(gx_peer(step), gy), device_id_type=MESH)

    lane = lax.broadcasted_iota(jnp.int32, (1, 128), 1)
    asked = jnp.zeros((1, 128), jnp.int32)
    inverse = jnp.zeros((1, 128), jnp.int32)
    rows = []
    for p in range(PAIR_DEV):
        first = image_slot[pairs[0, p]]
        second = image_slot[pairs[1, p]]
        row = second // (IMG_DEV * N_GY)
        rank = jnp.int32(0)
        for earlier in rows:
            rank = rank + jnp.where(earlier == row, 1, 0)
        rows.append(row)
        for view, slot, value in (
            (p, (first // IMG_DEV) % N_GY, first),
            (PAIR_DEV + p, N_GY + 2 * row + rank, second),
        ):
            source[view] = slot
            asked = jnp.where(lane == slot, IMG_DEV + value % IMG_DEV, asked)
            inverse = jnp.where(lane == slot, view, inverse)
    message[...] = asked
    got_message[gy] = asked
    got_message[N_GY + gx] = asked
    got_message[N_GY + N_GX] = inverse
    pl.semaphore_wait(barrier, N_GY - 1 + N_GX - 1)

    def message_copy(place, sender, device):
        return pltpu.make_async_remote_copy(
            src_ref=message,
            dst_ref=got_message.at[sender],
            send_sem=msg_send.at[place],
            recv_sem=msg_recv.at[sender],
            device_id=device,
            device_id_type=MESH,
        )

    for step in GY_STEPS:
        peer = gy_peer(step)
        message_copy(peer, gy, (gx, peer)).start()
    for step in GX_STEPS:
        peer = gx_peer(step)
        message_copy(N_GY + peer, N_GY + gx, (peer, gy)).start()

    loads[0].wait()
    loads[1].wait()
    half = 4 * PATCHES
    for part in range(2):
        value = jnp.dot(
            tokens[part * half : (part + 1) * half], w_embed[...], preferred_element_type=F32
        )
        for i in range(4):
            embedded[part * 4 + i, :PATCHES] = value[i * PATCHES : (i + 1) * PATCHES].astype(BF16)

    for step in GY_STEPS:
        peer = gy_peer(step)
        copy = message_copy(peer, peer, (gx, peer))
        copy.wait_send()
        copy.wait_recv()
    for step in GX_STEPS:
        peer = gx_peer(step)
        copy = message_copy(N_GY + peer, N_GY + peer, (peer, gy))
        copy.wait_send()
        copy.wait_recv()
    to_lists = pltpu.make_async_copy(got_message, lists, list_sem)
    to_lists.start()
    to_lists.wait()

    for slot in range(SLOTS):
        if slot < N_GY:
            value = lists[slot, 0, gy]
        else:
            value = lists[N_GY + (slot - N_GY) // 2, 0, N_GY + 2 * gx + slot % 2]
        asks[slot] = value % IMG_DEV
        table_out[slot] = value

    def slot_copies(part, forward):
        target = recv[part] if forward else back[part]
        sent, received = (fwd_send, fwd_recv) if forward else (bwd_send, bwd_recv)

        def gy_copy(peer, sender):
            return pltpu.make_async_remote_copy(
                src_ref=send[part].at[peer],
                dst_ref=target.at[sender],
                send_sem=sent.at[part, peer],
                recv_sem=received.at[part, sender],
                device_id=(gx, peer),
                device_id_type=MESH,
            )

        def gx_copy(peer, sender):
            return pltpu.make_async_remote_copy(
                src_ref=send[part].at[pl.ds(N_GY + 2 * peer, 2)],
                dst_ref=target.at[pl.ds(N_GY + 2 * sender, 2)],
                send_sem=sent.at[part, N_GY + peer],
                recv_sem=received.at[part, N_GY + sender],
                device_id=(peer, gy),
                device_id_type=MESH,
            )

        return gy_copy, gx_copy

    def start_copies(part, forward):
        gy_copy, gx_copy = slot_copies(part, forward)
        for i in range(max(len(GY_STEPS), len(GX_STEPS))):
            gy_copy(gy_peer(GY_STEPS[i]), gy).start()
            if i < len(GX_STEPS):
                gx_copy(gx_peer(GX_STEPS[i]), gx).start()

    def wait_copies(part, forward, what):
        gy_copy, gx_copy = slot_copies(part, forward)

        def wait(copy):
            if what == "send":
                copy.wait_send()
            else:
                copy.wait_recv()

        for step in GY_STEPS:
            peer = gy_peer(step)
            wait(gy_copy(peer, peer))
        for step in GX_STEPS:
            peer = gx_peer(step)
            wait(gx_copy(peer, peer))

    for part in OUTWARD:
        exact = slice(STARTS[part], STARTS[part] + SIZES[part])

        def pack(slot, carry):
            send[part][slot] = embedded[asks[slot], exact]
            return carry

        lax.fori_loop(0, SLOTS, pack, 0)
        start_copies(part, True)
        for slot in (gy, N_GY + 2 * gx, N_GY + 2 * gx + 1):
            recv[part][slot] = embedded[asks[slot], exact]
    for load in loads[2:]:
        load.wait()
    views[:, STARTS[-1] :] = jnp.zeros((2 * PAIR_DEV, PADDED[-1], D_MODEL), BF16)

    def project(part):
        wait_copies(part, True, "recv")
        size = PADDED[part]
        exact = slice(STARTS[part], STARTS[part] + SIZES[part])
        place = slice(STARTS[part], STARTS[part] + size)

        def side(group, carry):
            for p in range(PAIR_DEV):
                view = group * PAIR_DEV + p
                views[view, exact] = recv[part][source[view]]
            block = jnp.concatenate(
                [views[group * PAIR_DEV + p, place] for p in range(PAIR_DEV)], axis=0
            ).astype(F32)
            normal = normalize(block)
            normed_q = (normal * gain_query[...]).astype(BF16)
            normed_k = (normal * gain_key[...]).astype(BF16)
            for normed, weight, out, scale in (
                (normed_q, w_query, q_all, (D_MODEL // HEADS) ** -0.5),
                (normed_k, w_key, k_all, None),
                (normed_k, w_value, v_all, None),
            ):
                value = jnp.dot(normed, weight[...], preferred_element_type=F32)
                if scale is not None:
                    value = value * scale
                value = value.astype(BF16)
                for p in range(PAIR_DEV):
                    out[group * PAIR_DEV + p, place] = value[p * size : (p + 1) * size]
            return carry

        lax.fori_loop(0, 2, side, 0)

    for part in OUTWARD:
        project(part)

    def attend(part):
        size = PADDED[part]
        exact = slice(STARTS[part], STARTS[part] + SIZES[part])
        place = slice(STARTS[part], STARTS[part] + size)
        quad = 4 * (D_MODEL // HEADS)
        head_of = lax.broadcasted_iota(jnp.int32, (size, quad), 1) // (D_MODEL // HEADS)
        key_of = lax.broadcasted_iota(jnp.int32, (4 * size, ROWS), 1)
        at_once = 2 * GROUP if size <= 16 else GROUP

        def score(view, features):
            query = q_all[view, place, features]
            stacked = jnp.concatenate(
                [jnp.where(head_of == j, query, jnp.zeros_like(query)) for j in range(4)], axis=0
            )
            return lax.dot_general(
                stacked,
                k_all[(view + PAIR_DEV) % (2 * PAIR_DEV), :, features],
                (((1,), (1,)), ((), ())),
                preferred_element_type=F32,
            )

        def soften(scores):
            scores = jnp.where(key_of < PATCHES, scores, -jnp.inf)
            expd = jnp.exp(scores - jnp.max(scores, axis=-1, keepdims=True))
            return (expd * (1.0 / jnp.sum(expd, axis=-1, keepdims=True))).astype(BF16)

        def gather(view, features, weights):
            out = jnp.dot(
                weights,
                v_all[(view + PAIR_DEV) % (2 * PAIR_DEV), :, features],
                preferred_element_type=F32,
            )
            attended = out[:size]
            for j in range(1, 4):
                attended = jnp.where(head_of == j, out[j * size : (j + 1) * size], attended)
            mixed[view, :size, features] = attended.astype(BF16)

        def some_views(group, carry):
            items = [
                (group * at_once + i, slice(four * quad, (four + 1) * quad))
                for i in range(at_once)
                for four in range(HEADS // 4)
            ]
            weights = [soften(scores) for scores in [score(*item) for item in items]]
            for item, weight in zip(items, weights):
                gather(*item, weight)
            return carry

        lax.fori_loop(0, 2 * PAIR_DEV // at_once, some_views, 0)

        def side(group, carry):
            block = jnp.concatenate(
                [mixed[group * PAIR_DEV + p, :size] for p in range(PAIR_DEV)], axis=0
            )
            value = jnp.dot(block, w_out[...], preferred_element_type=F32)
            for p in range(PAIR_DEV):
                view = group * PAIR_DEV + p
                query = views[view, place].astype(F32)
                resid = (query + value[p * size : (p + 1) * size]).astype(BF16)
                views[view, place] = (normalize(resid.astype(F32)) * gain_head[...]).astype(BF16)
            return carry

        lax.fori_loop(0, 2, side, 0)

        wait_copies(part, True, "send")

        def pack(slot, carry):
            send[part][slot] = views[lists[N_GY + N_GX, 0, slot], exact]
            return carry

        lax.fori_loop(0, SLOTS, pack, 0)
        start_copies(part, False)
        for copy in self_copies(part):
            copy.start()

    def self_copies(part):
        return [
            pltpu.make_async_copy(send[part].at[place], back[part].at[place], self_sem.at[part, i])
            for i, place in enumerate([pl.ds(gy, 1), pl.ds(N_GY + 2 * gx, 2)])
        ]

    for part in HOMEWARD:
        attend(part)
    def leave(part):
        size = PADDED[part]
        return pltpu.make_async_copy(
            offered.at[:, pl.ds(0, size)],
            given.at[:, pl.ds(STARTS[part], size)],
            head_sem.at[PARTS + part],
        )

    def contribute(part, landed):
        size = PADDED[part]
        exact = slice(STARTS[part], STARTS[part] + SIZES[part])
        place = slice(STARTS[part], STARTS[part] + size)

        def some_slots(group, carry):
            for p in range(PAIR_DEV):
                views[p, exact] = landed[group * PAIR_DEV + p]
            normed = jnp.concatenate([views[p, place] for p in range(PAIR_DEV)], axis=0)
            raw = jnp.dot(normed, w_head[...], preferred_element_type=F32)
            confidence = 1.0 + jnp.exp(raw[:, 3 * PIXELS :])
            for plane in range(4):
                columns = slice(plane * PIXELS, (plane + 1) * PIXELS)
                value = confidence if plane == 3 else raw[:, columns] * confidence
                value = value.astype(BF16)
                for p in range(PAIR_DEV):
                    offered[group * PAIR_DEV + p, :size, columns] = value[p * size : (p + 1) * size]
            return carry

        lax.fori_loop(0, SLOTS // PAIR_DEV, some_slots, 0)

    previous = None
    for part in HOMEWARD:
        for copy in self_copies(part):
            copy.wait()
        wait_copies(part, False, "recv")
        landed = last_back
        if part != LAST:
            landed = recv[part]
            arrive = pltpu.make_async_copy(back[part], landed, head_sem.at[part])
            arrive.start()
            arrive.wait()
        if previous is not None:
            previous.wait()
        contribute(part, landed)
        previous = leave(part)
        previous.start()
    for part in HOMEWARD:
        wait_copies(part, False, "send")
    previous.wait()


def exchange(
    image_slot, pairs, tokens, w_embed, gain_query, gain_key, gain_head, w_query, w_key, w_value, w_out, w_head
):
    any_space = pl.BlockSpec(memory_space=pl.ANY)
    smem = pl.BlockSpec(memory_space=pltpu.SMEM)
    vmem = pl.BlockSpec(memory_space=pltpu.VMEM)
    square = pltpu.VMEM((D_MODEL, D_MODEL), BF16)
    full = pltpu.VMEM((2 * PAIR_DEV, ROWS, D_MODEL), BF16)
    return pl.pallas_call(
        exchange_kernel,
        out_shape=[
            jax.ShapeDtypeStruct((SLOTS, ROWS, HEAD_OUT), BF16),
            jax.ShapeDtypeStruct((SLOTS,), jnp.int32),
        ]
        + [
            jax.ShapeDtypeStruct((SLOTS, size, D_MODEL), BF16)
            for part, size in enumerate(SIZES)
            if part != LAST
        ],
        in_specs=[smem, smem, any_space, any_space, vmem, vmem, vmem] + [any_space] * 5,
        out_specs=[any_space, smem] + [any_space] * (PARTS - 1),
        scratch_shapes=[pltpu.VMEM((SLOTS, size, D_MODEL), BF16) for size in SIZES * 2]
        + [
            pltpu.VMEM((IMG_DEV * PATCHES, D_ENC), BF16),
            pltpu.VMEM((D_ENC, D_MODEL), BF16),
            square,
            square,
            square,
            square,
            pltpu.VMEM((D_MODEL, HEAD_OUT), BF16),
            pltpu.VMEM((SLOTS, SIZES[LAST], D_MODEL), BF16),
            pltpu.VMEM((SLOTS, max(PADDED), HEAD_OUT), BF16),
            pltpu.VMEM((IMG_DEV, ROWS, D_MODEL), BF16),
            full,
            full,
            full,
            full,
            pltpu.VMEM((2 * PAIR_DEV, max(PADDED), D_MODEL), BF16),
            pltpu.VMEM((1, 128), jnp.int32),
            pltpu.VMEM((N_GY + N_GX + 1, 1, 128), jnp.int32),
            pltpu.SMEM((N_GY + N_GX + 1, 1, 128), jnp.int32),
            pltpu.SMEM((2 * PAIR_DEV,), jnp.int32),
            pltpu.SMEM((SLOTS,), jnp.int32),
            pltpu.SemaphoreType.DMA((7,)),
            pltpu.SemaphoreType.DMA,
            pltpu.SemaphoreType.DMA((PARTS, 2)),
            pltpu.SemaphoreType.DMA((2 * PARTS,)),
            pltpu.SemaphoreType.DMA((N_GY + N_GX,)),
            pltpu.SemaphoreType.DMA((N_GY + N_GX,)),
            pltpu.SemaphoreType.DMA((PARTS, N_GY + N_GX)),
            pltpu.SemaphoreType.DMA((PARTS, N_GY + N_GX)),
            pltpu.SemaphoreType.DMA((PARTS, N_GY + N_GX)),
            pltpu.SemaphoreType.DMA((PARTS, N_GY + N_GX)),
        ],
        compiler_params=pltpu.CompilerParams(
            collective_id=0, has_side_effects=True, vmem_limit_bytes=62 * 2**20
        ),
        name="exchange",
    )(image_slot, pairs, tokens, w_embed, gain_query, gain_key, gain_head, w_query, w_key, w_value, w_out, w_head)


def sum_kernel(table, source, out, block, total, staged, first, order, sems, out_sems):
    def place_of(slot):
        return jnp.where(table[slot] >= IMG_DEV, (table[slot] % IMG_DEV) // 2, COUPLES)

    for couple in range(COUPLES + 1):
        first[couple] = 0

    def tally(slot, carry):
        couple = place_of(slot)
        first[couple] = first[couple] + 1
        return carry

    lax.fori_loop(0, SLOTS, tally, 0)
    bounds = [jnp.int32(0)]
    for couple in range(COUPLES):
        bounds.append(bounds[-1] + first[couple])
    for couple in range(COUPLES + 1):
        first[couple] = bounds[couple]

    def arrange(slot, carry):
        couple = place_of(slot)
        order[first[couple]] = slot
        first[couple] = first[couple] + 1
        return carry

    lax.fori_loop(0, SLOTS, arrange, 0)
    count = bounds[-1]

    def copy(item):
        place = item % DEPTH
        return pltpu.make_async_copy(source.at[order[item]], block.at[place], sems.at[place])

    def start(item):
        @pl.when(item < count)
        def _():
            copy(item).start()

    for item in range(DEPTH - 1):
        start(item)
    total[...] = jnp.zeros_like(total)

    def one_item(item, carry):
        start(item + DEPTH - 1)
        copy(item).wait()
        total[table[order[item]] % IMG_DEV] += block[item % DEPTH].astype(F32)
        return carry

    leaving = []
    for couple in range(COUPLES):
        lax.fori_loop(bounds[couple], bounds[couple + 1], one_item, 0)
        for image in (2 * couple, 2 * couple + 1):
            staged[image * PATCHES : (image + 1) * PATCHES] = total[image, :PATCHES]
        rows = slice(2 * couple * PATCHES, 2 * (couple + 1) * PATCHES)
        leaving.append(pltpu.make_async_copy(staged.at[rows], out.at[rows], out_sems.at[couple]))
        leaving[-1].start()
    for parting in leaving:
        parting.wait()


def sum_slots(table, contributions):
    any_space = pl.BlockSpec(memory_space=pl.ANY)
    return pl.pallas_call(
        sum_kernel,
        out_shape=jax.ShapeDtypeStruct((IMG_DEV * PATCHES, HEAD_OUT), F32),
        in_specs=[pl.BlockSpec(memory_space=pltpu.SMEM), any_space],
        out_specs=any_space,
        scratch_shapes=[
            pltpu.VMEM((DEPTH, ROWS, HEAD_OUT), BF16),
            pltpu.VMEM((IMG_DEV, ROWS, HEAD_OUT), F32),
            pltpu.VMEM((IMG_DEV * PATCHES, HEAD_OUT), F32),
            pltpu.SMEM((COUPLES + 1,), jnp.int32),
            pltpu.SMEM((SLOTS,), jnp.int32),
            pltpu.SemaphoreType.DMA((DEPTH,)),
            pltpu.SemaphoreType.DMA((COUPLES,)),
        ],
        compiler_params=pltpu.CompilerParams(vmem_limit_bytes=60 * 2**20),
        name="sum_slots",
    )(table, contributions)


def per_device(
    tokens,
    image_slot,
    pairs,
    w_embed,
    gain_query,
    gain_key,
    w_query,
    w_key,
    w_value,
    w_out,
    gain_head,
    w_head,
):
    contributions, table, *_ = exchange(
        image_slot,
        pairs.T,
        tokens,
        w_embed,
        gain_query,
        gain_key,
        gain_head,
        w_query,
        w_key,
        w_value,
        w_out,
        w_head,
    )
    return sum_slots(table, contributions)


def solution(mesh):
    split = P(("gx", "gy"), None)
    return jax.shard_map(
        per_device,
        mesh=mesh,
        in_specs=(split, P(), split) + (P(),) * 9,
        out_specs=split,
        check_vma=False,
    )
```
